256 devices in a mesh: section: 8 (over x, core), expert: 32 (over z, y).
Axes of the slice: x: 4, y: 4, z: 8, core: 2. Of those that a mesh axis runs over, the one named last changes fastest.
Arguments:
- tokens_fwd: bfloat16 [8, 3072, 4096], P('section', 'expert'), may hold values from -6 to 6
- expert_ids_fwd: int32 [8, 3072, 2], P('section', 'expert'), may hold values from 0 to 15, all different within a row; in each aligned block of 96 rows (0 to 95, 96 to 191, ..., all dimensions but the last counted through in order) at most 16 rows name the same one
- route_weights_fwd: float32 [8, 3072, 2], P('section', 'expert'), may hold values from 0.2 to 1
- tokens_bwd: bfloat16 [8, 3072, 4096], P('section', 'expert'), may hold values from -6 to 6
- cotangent: bfloat16 [8, 3072, 4096], P('section', 'expert'), may hold values from -6 to 6
- expert_ids_bwd: int32 [8, 3072, 2], P('section', 'expert'), may hold values from 0 to 15, all different within a row; in each aligned block of 96 rows (0 to 95, 96 to 191, ..., all dimensions but the last counted through in order) at most 16 rows name the same one
- route_weights_bwd: float32 [8, 3072, 2], P('section', 'expert'), may hold values from 0.2 to 1
- w_gate: bfloat16 [8, 4096, 12288], P('section', None, 'expert'), may hold values from -0.09375 to 0.09375
- w_up: bfloat16 [8, 4096, 12288], P('section', None, 'expert'), may hold values from -0.09375 to 0.09375
- w_down: bfloat16 [8, 12288, 4096], P('section', 'expert'), may hold values from -0.21875 to 0.21875
Outputs:
- next_input: bfloat16 [8, 3072, 4096], P('section', 'expert')
- prev_grad: bfloat16 [8, 3072, 4096], P('section', 'expert')
The draws below stay inside these ranges and needn't reach their ends.
Inputs may be any that keep to these rules, and one draw needn't show every extreme that they name: `expert_ids_fwd`: each token names 2 different experts. Within the 96 tokens of one index of expert at one section, no expert is named more than 16 times, a bound that some block reaches. `expert_ids_bwd`: as for expert_ids_fwd.
All inputs are finite; a program needn't handle non-finite values.
Results may differ from the reference program's by a relative error of at most 0.0035.
Values may be sent and summed in bfloat16 or wider, within the bound.
A program may use at most 128 MiB of HBM per device.

```python
import math
import jax
import jax.numpy as jnp
import numpy as np
from jax import lax

D = 4096
FFW = 768
TOP = 2
TOK_DEV = 96
SECTIONS = 8
EXPERTS = 16
TOKENS = 3072
CAP = 16
N_EXPERT = 32


def shard_levels(rng, shape, shards, low, top_value):
    factor_of = 1.0
    for position, parts in shards:
        heights = jax.random.uniform(jax.random.fold_in(jax.random.fold_in(rng, 6), position), (parts,), jnp.float32, low / len(shards), top_value / len(shards))
        factor_of = factor_of * jnp.repeat(jnp.exp(heights), shape[position] // parts).reshape((-1,) + (1,) * (len(shape) - 1 - position))
    return factor_of


def routed_block(rng, own, number, rows, number_of, top, most, skew):
    sequence = jax.random.permutation(rng, number_of)
    heavy_load, usual = shares(number_of, rows * top, most, skew, True), shares(number_of, rows * top, most, skew, False)
    places = jnp.arange(number_of)

    def named(tallies, rotation):
        used = int((tallies > 0).sum())
        fixed = max(1, used // 4)
        moved = fixed + (places - fixed + rotation * (used - fixed)) % max(1, number_of - fixed)
        return jnp.zeros((number_of,), jnp.int32).at[sequence[jnp.where(places < fixed, places, moved)]].set(jnp.asarray(tallies, jnp.int32))

    tallies = jnp.where(number % 4 == 0, named(heavy_load, number // 4), named(usual, number - number // 4 - 1))
    mixed = jax.random.permutation(jax.random.fold_in(own, 3), number_of)
    giver, receiver = mixed[0:number_of // 2 * 2:2], mixed[1:number_of // 2 * 2:2]
    room = jnp.minimum(tallies[giver] - 1, most - tallies[receiver]) // 2
    room = jnp.where((giver == sequence[0]) | (receiver == sequence[0]) | (tallies[receiver] == 0), 0, jnp.maximum(room, 0))
    moved = jax.random.randint(jax.random.fold_in(own, 4), (number_of // 2,), 0, 1 << 20) % (room + 1)
    tallies = tallies.at[giver].add(-moved).at[receiver].add(moved)
    labels = jnp.searchsorted(jnp.cumsum(tallies), jnp.arange(rows * top), side="right").astype(jnp.int32)
    listing = labels.reshape(top, rows).T
    listing = listing[jax.random.permutation(jax.random.fold_in(own, 1), rows)]
    rotation = jax.random.randint(jax.random.fold_in(own, 2), (rows, 1), 0, top)
    return jnp.take_along_axis(listing, (jnp.arange(top)[None, :] + rotation) % top, axis=1)


def shares(amount, total, limit, skew, full):
    loads = [(1 << 20) // math.isqrt(rank ** skew) + 1 for rank in range(1, amount + 1)]
    largest = limit if full else min(limit, max(-(-total // amount), total * loads[0] // sum(loads)))
    least = 1 if total - largest >= amount - 1 else 0
    holding, spare = [largest] + [least] * (amount - 1), total - largest - least * (amount - 1)
    while spare > 0:
        free = [i for i in range(1, amount) if holding[i] < largest] or [i for i in range(1, amount) if holding[i] < limit]
        whole, left = sum([loads[i] for i in free]), spare
        for i in free:
            addition = min(limit - holding[i], max(1, left * loads[i] // whole), spare)
            holding[i] = holding[i] + addition
            spare = spare - addition
    return np.array(holding)


def centred(stream_key, extent, scale, reach, cuts=(), kind=jnp.bfloat16):
    result = scale * jax.random.normal(stream_key, extent, jnp.float32)
    if cuts:
        result = result * shard_levels(stream_key, extent, cuts, -0.22, 0.18)
    return jnp.clip(result, -reach, reach).astype(kind)


def setup_inputs(seed: int = 0) -> dict:
    key_list = jax.random.split(jax.random.key(seed), 11)
    tokens_fwd = centred(key_list[0], (SECTIONS, TOKENS, D), 1.0, 6.0, ((0, 8), (1, 32)))
    expert_ids_fwd_keys = jax.random.split(jax.random.fold_in(key_list[1], 1), SECTIONS * TOKENS // TOK_DEV)
    expert_ids_fwd_turns = jax.random.permutation(jax.random.fold_in(key_list[1], 3), SECTIONS * TOKENS // TOK_DEV)
    expert_ids_fwd = jax.vmap(lambda own, number: routed_block(jax.random.fold_in(key_list[1], 2), own, number, TOK_DEV, EXPERTS, TOP, CAP, 2))(expert_ids_fwd_keys, expert_ids_fwd_turns).reshape((SECTIONS, TOKENS, TOP))
    route_weights_fwd = jnp.clip(0.2 + 0.8 * jax.random.uniform(key_list[2], (SECTIONS, TOKENS, TOP), jnp.float32) ** shard_levels(key_list[2], (SECTIONS, TOKENS, TOP), ((0, 8), (1, 32)), -0.2, 0.2), 0.2, 1.0)
    tokens_bwd = centred(key_list[3], (SECTIONS, TOKENS, D), 1.0, 6.0, ((0, 8), (1, 32)))
    cotangent = centred(key_list[4], (SECTIONS, TOKENS, D), 1.0, 6.0, ((0, 8), (1, 32)))
    expert_ids_bwd_keys = jax.random.split(jax.random.fold_in(key_list[5], 1), SECTIONS * TOKENS // TOK_DEV)
    expert_ids_bwd_turns = jax.random.permutation(jax.random.fold_in(key_list[5], 3), SECTIONS * TOKENS // TOK_DEV)
    expert_ids_bwd = jax.vmap(lambda own, number: routed_block(jax.random.fold_in(key_list[5], 2), own, number, TOK_DEV, EXPERTS, TOP, CAP, 2))(expert_ids_bwd_keys, expert_ids_bwd_turns).reshape((SECTIONS, TOKENS, TOP))
    route_weights_bwd = jnp.clip(0.2 + 0.8 * jax.random.uniform(key_list[6], (SECTIONS, TOKENS, TOP), jnp.float32) ** shard_levels(key_list[6], (SECTIONS, TOKENS, TOP), ((0, 8), (1, 32)), -0.2, 0.2), 0.2, 1.0)
    w_gate = centred(key_list[7], (SECTIONS, D, EXPERTS * FFW), D ** -0.5, 0.09375, ((0, 8), (2, 32)))
    w_up = centred(key_list[8], (SECTIONS, D, EXPERTS * FFW), D ** -0.5, 0.09375, ((0, 8), (2, 32)))
    w_down = centred(key_list[9], (SECTIONS, EXPERTS * FFW, D), FFW ** -0.5, 0.21875, ((0, 8), (1, 32)))
    return {"tokens_fwd": tokens_fwd, "expert_ids_fwd": expert_ids_fwd, "route_weights_fwd": route_weights_fwd, "tokens_bwd": tokens_bwd, "cotangent": cotangent, "expert_ids_bwd": expert_ids_bwd, "route_weights_bwd": route_weights_bwd, "w_gate": w_gate, "w_up": w_up, "w_down": w_down}


def place_rows(expert_ids):
    blocks = expert_ids.reshape(N_EXPERT, TOK_DEV * TOP)
    onehot = (blocks[:, :, None] == jnp.arange(EXPERTS, dtype=jnp.int32)[None, None, :]).astype(jnp.int32)
    running = jnp.cumsum(onehot, axis=1)
    slot_of = jnp.sum(onehot * running, axis=2) - 1
    row_of = jnp.arange(N_EXPERT, dtype=jnp.int32)[:, None] * CAP + slot_of
    return blocks.reshape(-1), row_of.reshape(-1).astype(jnp.int32)


def fill_buffer(source, expert_ids):
    experts_of, rows_of = place_rows(expert_ids)
    owner_row = jnp.arange(TOKENS * TOP, dtype=jnp.int32) // TOP
    buffer = jnp.zeros((EXPERTS, N_EXPERT * CAP, source.shape[1]), source.dtype)
    return buffer.at[experts_of, rows_of].set(source[owner_row]), experts_of, rows_of


def weight_slices(expert_index, gate_all, up_all, down_all):
    first_col = (expert_index * FFW).astype(jnp.int32)
    gate_part = lax.dynamic_slice_in_dim(gate_all, first_col, FFW, 1)
    up_part = lax.dynamic_slice_in_dim(up_all, first_col, FFW, 1)
    down_part = lax.dynamic_slice_in_dim(down_all, first_col, FFW, 0)
    return gate_part, up_part, down_part


def forward_section(section_args):
    tokens, expert_ids, weights, gate_all, up_all, down_all = section_args
    buffer, experts_of, rows_of = fill_buffer(tokens, expert_ids)

    def one_expert(entry_pair):
        row_block, expert_index = entry_pair
        gate_part, up_part, down_part = weight_slices(expert_index, gate_all, up_all, down_all)
        gate_out = jnp.dot(row_block, gate_part, preferred_element_type=jnp.float32)
        up_out = jnp.dot(row_block, up_part, preferred_element_type=jnp.float32)
        hidden = (jax.nn.silu(gate_out) * up_out).astype(jnp.bfloat16)
        return jnp.dot(hidden, down_part, preferred_element_type=jnp.float32)

    outputs = lax.map(one_expert, (buffer, jnp.arange(EXPERTS, dtype=jnp.int32)))
    picked = outputs[experts_of, rows_of].reshape(TOKENS, TOP, D)
    combined = tokens.astype(jnp.float32) + jnp.sum(weights[:, :, None] * picked, axis=1)
    return combined.astype(jnp.bfloat16)


def backward_section(section_args):
    tokens, cotangent, expert_ids, weights, gate_all, up_all, down_all = section_args
    stacked = jnp.concatenate([tokens, cotangent], axis=1)
    buffer, experts_of, rows_of = fill_buffer(stacked, expert_ids)

    def one_expert(entry_pair):
        row_block, expert_index = entry_pair
        gate_part, up_part, down_part = weight_slices(expert_index, gate_all, up_all, down_all)
        inputs_part = row_block[:, :D]
        grads_part = row_block[:, D:]
        gate_out = jnp.dot(inputs_part, gate_part, preferred_element_type=jnp.float32)
        up_out = jnp.dot(inputs_part, up_part, preferred_element_type=jnp.float32)
        sigmoid_val = jax.nn.sigmoid(gate_out)
        activated = gate_out * sigmoid_val
        act_slope = sigmoid_val * (1.0 + gate_out * (1.0 - sigmoid_val))
        grad_hidden = jnp.dot(grads_part, down_part.T, preferred_element_type=jnp.float32)
        grad_gate = (grad_hidden * up_out * act_slope).astype(jnp.bfloat16)
        grad_up = (grad_hidden * activated).astype(jnp.bfloat16)
        pulled = jnp.dot(grad_gate, gate_part.T, preferred_element_type=jnp.float32)
        return pulled + jnp.dot(grad_up, up_part.T, preferred_element_type=jnp.float32)

    outputs = lax.map(one_expert, (buffer, jnp.arange(EXPERTS, dtype=jnp.int32)))
    picked = outputs[experts_of, rows_of].reshape(TOKENS, TOP, D)
    combined = cotangent.astype(jnp.float32) + jnp.sum(weights[:, :, None] * picked, axis=1)
    return combined.astype(jnp.bfloat16)


def reference(tokens_fwd, expert_ids_fwd, route_weights_fwd, tokens_bwd, cotangent, expert_ids_bwd, route_weights_bwd, w_gate, w_up, w_down):
    layer_out = lax.map(forward_section, (tokens_fwd, expert_ids_fwd, route_weights_fwd, w_gate, w_up, w_down))
    input_grad = lax.map(backward_section, (tokens_bwd, cotangent, expert_ids_bwd, route_weights_bwd, w_gate, w_up, w_down))
    return jnp.roll(layer_out, 1, axis=0), jnp.roll(input_grad, -1, axis=0)
```

```python
import functools

import jax
import jax.numpy as jnp
from jax import lax
from jax.experimental import pallas as pl
from jax.experimental.pallas import tpu as pltpu
from jax.sharding import PartitionSpec as P

MESH = pl.DeviceIdType.MESH
BF16 = jnp.bfloat16
F32 = jnp.float32

WIDTH = 4096
HIDDEN = 384
TOK = 96
CAP = 16
SECTIONS = 8
LONG = 8
SHORT = 4
GROUPS = 4
COLS = 512
STEPS = WIDTH // COLS
NT = (((1,), (1,)), ((), ()))
TN = (((0,), (0,)), ((), ()))

OTHER, OWN, ACROSS, PARTNER, DIAGONAL = range(5)

AT_FORWARD, AT_RECOMPUTE, AT_BACKWARD = 2, 6, 10
AT_SUM = (6, 12)
AT_RETURN = (9, 13)
SLOTS = AT_RETURN[1] + GROUPS


def kernel(
    tok_f,
    tok_b,
    cot,
    meta_f,
    meta_b,
    gate_hbm,
    up_hbm,
    down_hbm,
    out_f,
    out_b,
    source,
    pack,
    rows,
    part_f,
    part_in,
    part_own,
    sums,
    back,
    w_gate,
    w_up,
    w_down,
    factors,
    pick,
    load_sem,
    z_send,
    z_recv,
    own_send,
    own_recv,
    other_send,
    other_recv,
    relay_send,
    relay_recv,
    part_send,
    part_recv,
    sum_send,
    sum_recv,
    back_send,
    back_recv,
    out_send,
    out_recv,
):
    section = lax.axis_index("section")
    expert = lax.axis_index("expert")
    z, y = expert // SHORT, expert % SHORT
    base = expert - y
    pair = y // 2
    partner = {"expert": base + (y + 1 - 2 * (y % 2))}
    across = {"expert": base + (SHORT - 1 - y)}

    def along_z(offset):
        return {"expert": lax.rem(z + offset, LONG) * SHORT + y}

    def along_sections(offset):
        return {"section": lax.rem(section + offset, SECTIONS)}

    loads = [
        pltpu.make_async_copy(tok_f.at[0], source.at[0], load_sem.at[0]),
        pltpu.make_async_copy(tok_b.at[0], source.at[1], load_sem.at[1]),
        pltpu.make_async_copy(cot.at[0], source.at[2], load_sem.at[2]),
        pltpu.make_async_copy(gate_hbm.at[0], w_gate, load_sem.at[3]),
        pltpu.make_async_copy(up_hbm.at[0], w_up, load_sem.at[4]),
        pltpu.make_async_copy(down_hbm.at[0], w_down, load_sem.at[5]),
    ]
    for load in loads:
        load.start()

    barrier = pltpu.get_barrier_semaphore()
    peers = [along_z(offset) for offset in range(1, LONG)]
    peers += [partner, across, along_sections(1), along_sections(SECTIONS - 1)]
    for peer in peers:
        pl.semaphore_signal(barrier, inc=1, device_id=peer, device_id_type=MESH)

    def z_copy(unit, group, side):
        place = 2 * group + side
        offset = group + 1 if side == 0 else LONG - 1 - group
        return pltpu.make_async_remote_copy(
            pack.at[unit, :, place],
            rows.at[unit, pl.ds(OTHER, 2), place],
            z_send.at[unit, place],
            z_recv.at[unit, place],
            device_id=along_z(offset),
            device_id_type=MESH,
        )

    def y_copy(unit, group, plane, to_plane, send, recv, device):
        span = pl.ds(2 * group, 2)
        return pltpu.make_async_remote_copy(
            rows.at[unit, plane, span],
            rows.at[unit, to_plane, span],
            send.at[unit, group],
            recv.at[unit, group],
            device_id=device,
            device_id_type=MESH,
        )

    def own_copy(unit, group):
        return y_copy(unit, group, OWN, PARTNER, own_send, own_recv, partner)

    def other_copy(unit, group):
        return y_copy(unit, group, OTHER, ACROSS, other_send, other_recv, across)

    def relay_copy(unit, group):
        return y_copy(unit, group, ACROSS, DIAGONAL, relay_send, relay_recv, partner)

    def part_copy(batch, group):
        span = pl.ds(2 * group, 2)
        src = part_f.at[:, span] if batch == 0 else pack.at[1, :, span]
        return pltpu.make_async_remote_copy(
            src,
            part_in.at[batch, :, span],
            part_send.at[batch, group],
            part_recv.at[batch, group],
            device_id=partner,
            device_id_type=MESH,
        )

    def sum_copy(batch, group):
        span = pl.ds(2 * group, 2)
        return pltpu.make_async_remote_copy(
            pack.at[2 * batch, 0, span],
            sums.at[batch, OTHER, span],
            sum_send.at[batch, group],
            sum_recv.at[batch, group],
            device_id=across,
            device_id_type=MESH,
        )

    def back_copy(batch, group, side):
        place = 2 * group + side
        offset = LONG - 1 - group if side == 0 else group + 1
        return pltpu.make_async_remote_copy(
            sums.at[batch, :, place],
            back.at[batch, :, place],
            back_send.at[batch, place],
            back_recv.at[batch, place],
            device_id=along_z(offset),
            device_id_type=MESH,
        )

    def out_copy(batch, step):
        cols = pl.ds(pl.multiple_of(step * COLS, COLS), COLS)
        out = out_f if batch == 0 else out_b
        return pltpu.make_async_remote_copy(
            source.at[2 * batch, :, cols],
            out.at[0, :, cols],
            out_send.at[batch, step],
            out_recv.at[batch, step],
            device_id=along_sections(1 if batch == 0 else SECTIONS - 1),
            device_id_type=MESH,
        )

    def both_sides(group, action):
        action(0)
        pl.when(group < GROUPS - 1)(lambda: action(1))

    def route(batch, meta):
        lanes = lax.broadcasted_iota(jnp.int32, (TOK, 128), 1)
        lane_f = lanes.astype(F32)
        first = (meta[:, 0:1] == lane_f).astype(F32)
        second = (meta[:, 1:2] == lane_f).astype(F32)
        earlier = (
            lax.broadcasted_iota(jnp.int32, (TOK, TOK), 0)
            > lax.broadcasted_iota(jnp.int32, (TOK, TOK), 1)
        ).astype(F32)
        rank = jnp.dot(
            earlier.astype(BF16), (first + second).astype(BF16), preferred_element_type=F32
        )
        ahead = (lanes >> 1) - z
        ahead = jnp.where(ahead < 0, ahead + LONG, ahead)
        place = jnp.where(ahead > 4, 2 * (LONG - ahead) - 1, 2 * ahead - 2)
        place = jnp.where(ahead == 0, LONG - 1, place)
        plane = jnp.where((lanes & 1) == pair, OWN, OTHER)
        slots = (plane * (LONG * CAP) + place * CAP).astype(F32) + rank
        wide = lax.broadcasted_iota(jnp.int32, (TOK, 2 * LONG * CAP), 1).astype(F32)
        for k, chosen in enumerate((first, second)):
            slot = jnp.sum(chosen * slots, axis=1, keepdims=True)
            pick[batch, k] = (slot == wide).astype(BF16)

    def pack_rows(unit):
        batch = 0 if unit == 0 else 1
        table = (pick[batch, 0].astype(F32) + pick[batch, 1].astype(F32)).T.astype(BF16)

        def step(i, _):
            cols = pl.ds(pl.multiple_of(i * COLS, COLS), COLS)
            packed = jnp.dot(table, source[unit, :, cols], preferred_element_type=F32)
            packed = packed.astype(BF16).reshape(2, LONG, CAP, COLS)
            pack[unit, :, :, :, cols] = packed
            rows[unit, OTHER : OWN + 1, LONG - 1, :, cols] = packed[:, LONG - 1]
            return 0

        lax.fori_loop(0, STEPS, step, 0)

    loads[0].wait()
    route(0, meta_f)
    pack_rows(0)
    pl.semaphore_wait(barrier, len(peers))
    for group in range(GROUPS):
        for side in range(2 if group < GROUPS - 1 else 1):
            z_copy(0, group, side).start()
    loads[1].wait()
    loads[2].wait()
    route(1, meta_b)
    pack_rows(1)
    pack_rows(2)
    for load in loads[3:]:
        load.wait()

    def expert_rows(unit, group):
        block = rows[unit, OWN : DIAGONAL + 1, pl.ds(2 * group, 2)]
        return block.reshape(4 * 2 * CAP, WIDTH)

    def wait_rows(unit, group):
        own_copy(unit, group).wait_recv()
        relay_copy(unit, group).wait_recv()

    def keep_partial(value, group, part, cols):
        span = pl.ds(2 * group, 2)
        value = value.reshape(2, 2, 2, CAP, COLS)
        part[:, span, :, cols] = value[1].astype(BF16)
        part_own[:, span, :, cols] = value[0]

    def forward(group):
        wait_rows(0, group)
        block = expert_rows(0, group)
        gate = jnp.dot(block, w_gate[...], preferred_element_type=F32)
        up = jnp.dot(block, w_up[...], preferred_element_type=F32)
        hidden = (gate * jax.nn.sigmoid(gate) * up).astype(BF16)

        def step(i, _):
            cols = pl.ds(pl.multiple_of(i * COLS, COLS), COLS)
            value = jnp.dot(hidden, w_down[:, cols], preferred_element_type=F32)
            keep_partial(value, group, part_f, cols)
            return 0

        lax.fori_loop(0, STEPS, step, 0)
        part_copy(0, group).start()

    def recompute(group):
        wait_rows(1, group)
        block = expert_rows(1, group)
        gate = jnp.dot(block, w_gate[...], preferred_element_type=F32)
        up = jnp.dot(block, w_up[...], preferred_element_type=F32)
        q = jax.nn.sigmoid(gate)
        factors[0, group] = up * (q * (1.0 + gate * (1.0 - q)))
        factors[1, group] = gate * q

    def backward(group):
        wait_rows(2, group)
        both_sides(group, lambda side: z_copy(1, group, side).wait_send())
        block = expert_rows(2, group)
        grad = lax.dot_general(block, w_down[...], NT, preferred_element_type=F32)
        grad_gate = (grad * factors[0, group]).astype(BF16)
        grad_up = (grad * factors[1, group]).astype(BF16)

        def step(i, _):
            cols = pl.ds(pl.multiple_of(i * COLS, COLS), COLS)
            value = lax.dot_general(grad_gate, w_gate[cols, :], NT, preferred_element_type=F32)
            value += lax.dot_general(grad_up, w_up[cols, :], NT, preferred_element_type=F32)
            keep_partial(value, group, pack.at[1], cols)
            return 0

        lax.fori_loop(0, STEPS, step, 0)
        part_copy(1, group).start()

    def add_partials(batch, group):
        part_copy(batch, group).wait_recv()
        both_sides(group, lambda side: z_copy(2 * batch, group, side).wait_send())
        span = pl.ds(2 * group, 2)

        def step(i, _):
            cols = pl.ds(pl.multiple_of(i * COLS, COLS), COLS)
            total = part_own[:, span, :, cols] + part_in[batch, :, span, :, cols].astype(F32)
            sums[batch, OWN, span, :, cols] = total[0].astype(BF16)
            pack[2 * batch, 0, span, :, cols] = total[1].astype(BF16)
            return 0

        lax.fori_loop(0, STEPS, step, 0)
        sum_copy(batch, group).start()

    def send_back(batch, group):
        sum_copy(batch, group).wait_recv()
        both_sides(group, lambda side: back_copy(batch, group, side).start())

        @pl.when(group == GROUPS - 1)
        def _():
            back[batch, :, LONG - 1] = sums[batch, :, LONG - 1]

    def slot(t, _):
        def at(first, count, action):
            @pl.when((t >= first) & (t < first + count))
            def _():
                action(t - first)

        def arrivals(item):
            unit, group = item // GROUPS, item % GROUPS
            both_sides(group, lambda side: z_copy(unit, group, side).wait_recv())
            own_copy(unit, group).start()
            other_copy(unit, group).start()

            @pl.when(unit < 2)
            def _():
                both_sides(group, lambda side: z_copy(unit + 1, group, side).start())

        def relay(item):
            unit, group = item // GROUPS, item % GROUPS
            other_copy(unit, group).wait_recv()
            relay_copy(unit, group).start()

        at(0, 3 * GROUPS, arrivals)
        at(1, 3 * GROUPS, relay)
        at(AT_FORWARD, GROUPS, forward)
        at(AT_RECOMPUTE, GROUPS, recompute)
        at(AT_BACKWARD, GROUPS, backward)
        for batch in range(2):
            at(AT_SUM[batch], GROUPS, functools.partial(add_partials, batch))
            at(AT_RETURN[batch], GROUPS, functools.partial(send_back, batch))
        return 0

    lax.fori_loop(0, SLOTS, slot, 0)

    def finish(batch, meta):
        for place in range(LONG - 1):
            back_copy(batch, place // 2, place % 2).wait_recv()

        def step(i, _):
            cols = pl.ds(pl.multiple_of(i * COLS, COLS), COLS)
            returned = back[batch, :, :, :, cols].reshape(2 * LONG * CAP, COLS)
            first = jnp.dot(pick[batch, 0], returned, preferred_element_type=F32)
            second = jnp.dot(pick[batch, 1], returned, preferred_element_type=F32)
            total = meta[:, 2:3] * first + meta[:, 3:4] * second
            total += source[2 * batch, :, cols].astype(F32)
            source[2 * batch, :, cols] = total.astype(BF16)
            out_copy(batch, i).start()
            return 0

        lax.fori_loop(0, STEPS, step, 0)

    finish(0, meta_f)
    finish(1, meta_b)

    def drain(unit, _):
        def of_group(group, _):
            own_copy(unit, group).wait_send()
            other_copy(unit, group).wait_send()
            relay_copy(unit, group).wait_send()
            return 0

        return lax.fori_loop(0, GROUPS, of_group, 0)

    lax.fori_loop(0, 3, drain, 0)
    for batch in range(2):
        for group in range(GROUPS):
            part_copy(batch, group).wait_send()
            sum_copy(batch, group).wait_send()
        for place in range(LONG - 1):
            back_copy(batch, place // 2, place % 2).wait_send()
        for step in range(STEPS):
            out_copy(batch, step).wait()


def body(
    tokens_fwd,
    expert_ids_fwd,
    route_weights_fwd,
    tokens_bwd,
    cotangent,
    expert_ids_bwd,
    route_weights_bwd,
    w_gate,
    w_up,
    w_down,
):
    def meta(expert_ids, route_weights):
        joined = jnp.concatenate([expert_ids[0].astype(F32), route_weights[0]], axis=1)
        return jnp.pad(joined, ((0, 0), (0, 124)))

    anywhere = pl.BlockSpec(memory_space=pl.ANY)
    vmem = pl.BlockSpec(memory_space=pltpu.VMEM)
    out = jax.ShapeDtypeStruct((1, TOK, WIDTH), BF16)
    block = (LONG, CAP, WIDTH)

    def sems(*shape):
        return [pltpu.SemaphoreType.DMA(shape), pltpu.SemaphoreType.DMA(shape)]

    return pl.pallas_call(
        kernel,
        out_shape=(out, out),
        in_specs=[anywhere, anywhere, anywhere, vmem, vmem, anywhere, anywhere, anywhere],
        out_specs=(anywhere, anywhere),
        scratch_shapes=[
            pltpu.VMEM((3, TOK, WIDTH), BF16),
            pltpu.VMEM((3, 2) + block, BF16),
            pltpu.VMEM((3, 5) + block, BF16),
            pltpu.VMEM((2,) + block, BF16),
            pltpu.VMEM((2, 2) + block, BF16),
            pltpu.VMEM((2,) + block, F32),
            pltpu.VMEM((2, 2) + block, BF16),
            pltpu.VMEM((2, 2) + block, BF16),
            pltpu.VMEM((WIDTH, HIDDEN), BF16),
            pltpu.VMEM((WIDTH, HIDDEN), BF16),
            pltpu.VMEM((HIDDEN, WIDTH), BF16),
            pltpu.VMEM((2, GROUPS, 8 * CAP, HIDDEN), F32),
            pltpu.VMEM((2, 2, TOK, 2 * LONG * CAP), BF16),
            pltpu.SemaphoreType.DMA((6,)),
            *sems(3, LONG),
            *sems(3, GROUPS),
            *sems(3, GROUPS),
            *sems(3, GROUPS),
            *sems(2, GROUPS),
            *sems(2, GROUPS),
            *sems(2, LONG),
            *sems(2, STEPS),
        ],
        compiler_params=pltpu.CompilerParams(
            collective_id=0, has_side_effects=True, vmem_limit_bytes=62 * 2**20
        ),
        name="relay_experts",
    )(
        tokens_fwd,
        tokens_bwd,
        cotangent,
        meta(expert_ids_fwd, route_weights_fwd),
        meta(expert_ids_bwd, route_weights_bwd),
        w_gate,
        w_up,
        w_down,
    )


def solution(mesh):
    rows = P("section", "expert", None)
    columns = P("section", None, "expert")
    in_specs = (rows,) * 7 + (columns, columns, rows)
    return jax.shard_map(
        body, mesh=mesh, in_specs=in_specs, out_specs=(rows, rows), check_vma=False
    )
```

```python
import jax
import jax.numpy as jnp
from jax import lax
from jax.experimental import pallas as pl
from jax.experimental.pallas import tpu as pltpu
from jax.sharding import PartitionSpec as P

MESH = pl.DeviceIdType.MESH
BF16 = jnp.bfloat16
F32 = jnp.float32

WIDTH = 4096
HIDDEN = 384
TOK = 96
CAP = 16
SECTIONS = 8
LONG = 8
SHORT = 4
GROUPS = 4
COLS = 512
STEPS = WIDTH // COLS
NT = (((1,), (1,)), ((), ()))

OTHER, OWN, ACROSS, PARTNER, DIAGONAL = range(5)

PACK, SEND, ARRIVE, RELAY, FORWARD, RECOMPUTE, BACKWARD, PARTIAL, SUM, BACK, FINISH = range(11)
ORDER = (
    (ARRIVE, 0, 0), (SEND, 0, 1), (SEND, 0, 4), (PACK, 1), (ARRIVE, 1, 0), (PACK, 2),
    (RELAY, 0, 0), (SEND, 0, 5), (SEND, 0, 3), (SEND, 0, 6), (SEND, 0, 2), (SEND, 0, 7),
    (ARRIVE, 2, 0), (RELAY, 1, 0), (ARRIVE, 0, 1), (SEND, 1, 5), (SEND, 1, 6), (RELAY, 2, 0),
    (RELAY, 0, 1), (ARRIVE, 0, 4), (RELAY, 0, 4), (FORWARD, 0), (PARTIAL, 0, 0), (PARTIAL, 0, 1),
    (ARRIVE, 0, 5), (SEND, 2, 5), (SEND, 2, 6), (ARRIVE, 0, 6), (RELAY, 0, 5), (RELAY, 0, 6),
    (SUM, 0, 0), (ARRIVE, 0, 3), (ARRIVE, 0, 2), (BACK, 0, 0), (SUM, 0, 1), (RELAY, 0, 3),
    (SEND, 1, 3), (SEND, 1, 4), (RELAY, 0, 2), (ARRIVE, 0, 7), (BACK, 0, 1), (FORWARD, 2),
    (PARTIAL, 0, 4), (PARTIAL, 0, 5), (RELAY, 0, 7), (SEND, 2, 4), (SEND, 2, 7), (FORWARD, 1),
    (PARTIAL, 0, 3), (PARTIAL, 0, 2), (ARRIVE, 1, 5), (ARRIVE, 1, 6), (RELAY, 1, 5), (SEND, 1, 7),
    (SUM, 0, 4), (RELAY, 1, 6), (BACK, 0, 4), (SUM, 0, 5), (FORWARD, 3), (PARTIAL, 0, 6),
    (PARTIAL, 0, 7), (ARRIVE, 2, 5), (ARRIVE, 2, 6), (SEND, 2, 3), (BACK, 0, 5), (SUM, 0, 3),
    (RELAY, 2, 5), (RELAY, 2, 6), (SUM, 0, 2), (ARRIVE, 1, 4), (ARRIVE, 1, 3), (BACK, 0, 3),
    (BACK, 0, 2), (RELAY, 1, 4), (RELAY, 1, 3), (ARRIVE, 2, 4), (SEND, 1, 2), (RELAY, 2, 4),
    (SUM, 0, 6), (SEND, 2, 2), (BACK, 0, 6), (SUM, 0, 7), (ARRIVE, 2, 7), (BACK, 0, 7),
    (RELAY, 2, 7), (ARRIVE, 1, 7), (RELAY, 1, 7), (ARRIVE, 2, 3), (SEND, 1, 1), (RECOMPUTE, 2),
    (RELAY, 2, 3), (SEND, 2, 1), (BACKWARD, 2), (PARTIAL, 1, 5), (PARTIAL, 1, 4), (ARRIVE, 1, 2),
    (RELAY, 1, 2), (RECOMPUTE, 3), (ARRIVE, 2, 2), (BACKWARD, 3), (PARTIAL, 1, 6), (PARTIAL, 1, 7),
    (RELAY, 2, 2), (SUM, 1, 5), (BACK, 1, 5), (SUM, 1, 4), (BACK, 1, 4), (RECOMPUTE, 1),
    (ARRIVE, 1, 1), (RELAY, 1, 1), (ARRIVE, 2, 1), (FINISH, 0), (SUM, 1, 6), (RELAY, 2, 1),
    (BACK, 1, 6), (SUM, 1, 7), (BACKWARD, 1), (PARTIAL, 1, 3), (PARTIAL, 1, 2), (BACK, 1, 7),
    (RECOMPUTE, 0), (BACKWARD, 0), (PARTIAL, 1, 1), (PARTIAL, 1, 0), (SUM, 1, 3), (BACK, 1, 3),
    (SUM, 1, 2), (BACK, 1, 2), (SUM, 1, 1), (BACK, 1, 1), (SUM, 1, 0), (BACK, 1, 0), (FINISH, 1),
)
ASIDE = 12


def kernel(
    tok_f,
    tok_b,
    cot,
    ids_f,
    ids_b,
    weights_f,
    weights_b,
    gate_hbm,
    up_hbm,
    down_hbm,
    out_f,
    out_b,
    source,
    pack,
    rows,
    part_f,
    part_in,
    part_own,
    sums,
    back,
    w_gate,
    w_up,
    w_down,
    factors,
    residual,
    ids_in_f,
    ids_in_b,
    weights_in_f,
    weights_in_b,
    load_sem,
    z_send,
    z_recv,
    own_send,
    own_recv,
    other_send,
    other_recv,
    relay_send,
    relay_recv,
    part_send,
    part_recv,
    sum_send,
    sum_recv,
    back_send,
    back_recv,
    aside_send,
    aside_recv,
    out_sem,
):
    section = lax.axis_index("section")
    expert = lax.axis_index("expert")
    z, y = expert // SHORT, expert % SHORT
    base = expert - y
    pair = y // 2
    partner = {"expert": base + (y + 1 - 2 * (y % 2))}
    across = {"expert": base + (SHORT - 1 - y)}

    def along_z(offset):
        return {"expert": lax.rem(z + offset, LONG) * SHORT + y}

    def next_section(batch, offset):
        ahead = 1 if batch == 0 else SECTIONS - 1
        return {"section": lax.rem(section + ahead, SECTIONS)} | along_z(offset)

    loads = [
        pltpu.make_async_copy(tok_f.at[0], source.at[0], load_sem.at[0]),
        pltpu.make_async_copy(tok_b.at[0], source.at[1], load_sem.at[1]),
        pltpu.make_async_copy(cot.at[0], source.at[2], load_sem.at[2]),
        pltpu.make_async_copy(gate_hbm.at[0], w_gate, load_sem.at[3]),
        pltpu.make_async_copy(up_hbm.at[0], w_up, load_sem.at[4]),
        pltpu.make_async_copy(down_hbm.at[0], w_down, load_sem.at[5]),
    ]
    for load in loads:
        load.start()

    barrier = pltpu.get_barrier_semaphore()
    peers = [along_z(offset) for offset in range(1, LONG)]
    peers += [partner, across]
    peers += [next_section(batch, offset) for batch in range(2) for offset in range(LONG)]
    for peer in peers:
        pl.semaphore_signal(barrier, inc=1, device_id=peer, device_id_type=MESH)

    def ahead_of(place):
        half = (place + 1) // 2
        return half + (place + 1) % 2 * (LONG - 2 * half)

    def z_copy(unit, place):
        return pltpu.make_async_remote_copy(
            pack.at[unit, :, place],
            rows.at[unit, pl.ds(OTHER, 2), place],
            z_send.at[unit, place],
            z_recv.at[unit, place],
            device_id=along_z(ahead_of(place)),
            device_id_type=MESH,
        )

    def y_copy(unit, place, plane, to_plane, send, recv, device):
        return pltpu.make_async_remote_copy(
            rows.at[unit, plane, place],
            rows.at[unit, to_plane, place],
            send.at[unit, place],
            recv.at[unit, place],
            device_id=device,
            device_id_type=MESH,
        )

    def own_copy(unit, place):
        return y_copy(unit, place, OWN, PARTNER, own_send, own_recv, partner)

    def other_copy(unit, place):
        return y_copy(unit, place, OTHER, ACROSS, other_send, other_recv, across)

    def relay_copy(unit, place):
        return y_copy(unit, place, ACROSS, DIAGONAL, relay_send, relay_recv, partner)

    def part_copy(batch, place):
        return pltpu.make_async_remote_copy(
            part_f.at[:, place] if batch == 0 else pack.at[1, :, place],
            part_in.at[batch, :, place],
            part_send.at[batch, place],
            part_recv.at[batch, place],
            device_id=partner,
            device_id_type=MESH,
        )

    def sum_copy(batch, place):
        return pltpu.make_async_remote_copy(
            pack.at[2 * batch, 0, place],
            sums.at[batch, OTHER, place],
            sum_send.at[batch, place],
            sum_recv.at[batch, place],
            device_id=across,
            device_id_type=MESH,
        )

    def back_copy(batch, place):
        return pltpu.make_async_remote_copy(
            sums.at[batch, :, place],
            back.at[batch, :, place],
            back_send.at[batch, place],
            back_recv.at[batch, place],
            device_id=next_section(batch, LONG - ahead_of(place)),
            device_id_type=MESH,
        )

    def aside_copies(batch):
        pairs = (
            ((tok_f, cot)[batch].at[0], residual.at[batch]),
            ((ids_f, ids_b)[batch], (ids_in_f, ids_in_b)[batch]),
            ((weights_f, weights_b)[batch], (weights_in_f, weights_in_b)[batch]),
        )
        return [
            pltpu.make_async_remote_copy(
                src,
                dst,
                aside_send.at[batch, i],
                aside_recv.at[batch, i],
                device_id=next_section(batch, 0),
                device_id_type=MESH,
            )
            for i, (src, dst) in enumerate(pairs)
        ]

    def out_copy(batch, step):
        cols = pl.ds(pl.multiple_of(step * COLS, COLS), COLS)
        return pltpu.make_async_copy(
            residual.at[batch, :, cols],
            (out_f, out_b)[batch].at[0, :, cols],
            out_sem.at[batch, step],
        )

    def tables(ids):
        names = lax.broadcasted_iota(jnp.int32, (SECTIONS * 2, TOK), 0)
        chosen = [(ids[k : k + 1, :] == names).astype(F32) for k in range(2)]
        earlier = lax.broadcasted_iota(jnp.int32, (TOK, TOK), 0) < lax.broadcasted_iota(
            jnp.int32, (TOK, TOK), 1
        )
        rank = jnp.dot(
            (chosen[0] + chosen[1]).astype(BF16),
            earlier.astype(F32).astype(BF16),
            preferred_element_type=F32,
        )
        ahead = (names >> 1) - z
        ahead = jnp.where(ahead < 0, ahead + LONG, ahead)
        place = jnp.where(ahead > 4, 2 * (LONG - ahead), 2 * ahead - 1)
        place = jnp.where(ahead == 0, 0, place)
        plane = jnp.where((names & 1) == pair, OWN, OTHER)
        slots = (plane * (LONG * CAP) + place * CAP).astype(F32) + rank
        every = lax.broadcasted_iota(jnp.int32, (2 * LONG * CAP, TOK), 0).astype(F32)
        return [
            (jnp.sum(hot * slots, axis=0, keepdims=True) == every).astype(F32) for hot in chosen
        ]

    def pack_rows(unit, table):
        def step(i, _):
            cols = pl.ds(pl.multiple_of(i * COLS, COLS), COLS)
            packed = jnp.dot(table, source[unit, :, cols], preferred_element_type=F32)
            packed = packed.astype(BF16).reshape(2, LONG, CAP, COLS)
            pack[unit, :, :, :, cols] = packed
            rows[unit, OTHER : OWN + 1, 0, :, cols] = packed[:, 0]
            return 0

        lax.fori_loop(0, STEPS, step, 0)

    loads[0].wait()
    pack_rows(0, sum(tables(ids_f)).astype(BF16))
    pl.semaphore_wait(barrier, len(peers))

    def expert_rows(unit, group):
        block = rows[unit, OWN : DIAGONAL + 1, pl.ds(2 * group, 2)]
        return block.reshape(4 * 2 * CAP, WIDTH)

    def pack_unit(unit):
        loads[unit].wait()
        pack_rows(unit, sum(tables(ids_b)).astype(BF16))

    def arrive(unit, place):
        if place > 0:
            z_copy(unit, place).wait_recv()
        own_copy(unit, place).start()
        other_copy(unit, place).start()

    def relay(unit, place):
        other_copy(unit, place).wait_recv()
        relay_copy(unit, place).start()

    def wait_rows(unit, group):
        for place in (2 * group, 2 * group + 1):
            own_copy(unit, place).wait_recv()
            relay_copy(unit, place).wait_recv()

    def keep_partial(value, group, part, cols):
        span = pl.ds(2 * group, 2)
        value = value.reshape(2, 2, 2, CAP, COLS)
        part[:, span, :, cols] = value[1].astype(BF16)
        part_own[:, span, :, cols] = value[0]

    def forward(group):
        wait_rows(0, group)
        block = expert_rows(0, group)
        gate = jnp.dot(block, w_gate[...], preferred_element_type=F32)
        up = jnp.dot(block, w_up[...], preferred_element_type=F32)
        hidden = (gate * jax.nn.sigmoid(gate) * up).astype(BF16)

        def step(i, _):
            cols = pl.ds(pl.multiple_of(i * COLS, COLS), COLS)
            value = jnp.dot(hidden, w_down[:, cols], preferred_element_type=F32)
            keep_partial(value, group, part_f, cols)
            return 0

        lax.fori_loop(0, STEPS, step, 0)

    def recompute(group):
        wait_rows(1, group)
        block = expert_rows(1, group)
        gate = jnp.dot(block, w_gate[...], preferred_element_type=F32)
        up = jnp.dot(block, w_up[...], preferred_element_type=F32)
        q = jax.nn.sigmoid(gate)
        factors[0, group] = up * (q * (1.0 + gate * (1.0 - q)))
        factors[1, group] = gate * q

    def packed_has_left(unit, place):
        if place > 0:
            z_copy(unit, place).wait_send()

    def backward(group):
        wait_rows(2, group)
        packed_has_left(1, 2 * group)
        packed_has_left(1, 2 * group + 1)
        block = expert_rows(2, group)
        grad = lax.dot_general(block, w_down[...], NT, preferred_element_type=F32)
        grad_gate = (grad * factors[0, group]).astype(BF16)
        grad_up = (grad * factors[1, group]).astype(BF16)

        def step(i, _):
            cols = pl.ds(pl.multiple_of(i * COLS, COLS), COLS)
            value = lax.dot_general(grad_gate, w_gate[cols, :], NT, preferred_element_type=F32)
            value += lax.dot_general(grad_up, w_up[cols, :], NT, preferred_element_type=F32)
            keep_partial(value, group, pack.at[1], cols)
            return 0

        lax.fori_loop(0, STEPS, step, 0)

    def add_partials(batch, place):
        part_copy(batch, place).wait_recv()
        packed_has_left(2 * batch, place)

        def step(i, _):
            cols = pl.ds(pl.multiple_of(i * COLS, COLS), COLS)
            total = part_own[:, place, :, cols] + part_in[batch, :, place, :, cols].astype(F32)
            sums[batch, OWN, place, :, cols] = total[0].astype(BF16)
            pack[2 * batch, 0, place, :, cols] = total[1].astype(BF16)
            return 0

        lax.fori_loop(0, STEPS, step, 0)
        sum_copy(batch, place).start()

    def send_back(batch, place):
        sum_copy(batch, place).wait_recv()
        back_copy(batch, place).start()

    def finish(batch):
        for copy in aside_copies(batch):
            copy.wait_recv()
        weights = (weights_in_f, weights_in_b)[batch]
        picks = [hot.T.astype(BF16) for hot in tables((ids_in_f, ids_in_b)[batch])]
        same = lax.broadcasted_iota(jnp.int32, (TOK, TOK), 0) == lax.broadcasted_iota(
            jnp.int32, (TOK, TOK), 1
        )
        scale = [
            jnp.sum(jnp.where(same, weights[k : k + 1, :], 0.0), axis=1, keepdims=True)
            for k in range(2)
        ]
        for place in range(LONG):
            back_copy(batch, place).wait_recv()

        def step(i, _):
            cols = pl.ds(pl.multiple_of(i * COLS, COLS), COLS)
            returned = back[batch, :, :, :, cols].reshape(2 * LONG * CAP, COLS)
            first = jnp.dot(picks[0], returned, preferred_element_type=F32)
            second = jnp.dot(picks[1], returned, preferred_element_type=F32)
            total = scale[0] * first + scale[1] * second
            total += residual[batch, :, cols].astype(F32)
            residual[batch, :, cols] = total.astype(BF16)
            out_copy(batch, i).start()
            return 0

        lax.fori_loop(0, STEPS, step, 0)

    run = {
        PACK: pack_unit,
        SEND: lambda unit, place: z_copy(unit, place).start(),
        ARRIVE: arrive,
        RELAY: relay,
        FORWARD: forward,
        RECOMPUTE: recompute,
        BACKWARD: backward,
        PARTIAL: lambda batch, place: part_copy(batch, place).start(),
        SUM: add_partials,
        BACK: send_back,
        FINISH: finish,
    }
    loaded = False
    for count, (kind, *which) in enumerate(ORDER):
        if kind in (FORWARD, RECOMPUTE) and not loaded:
            for load in loads[3:]:
                load.wait()
            loaded = True
        run[kind](*which)
        if count == ASIDE:
            for batch in range(2):
                for copy in aside_copies(batch):
                    copy.start()

    def drain(unit, _):
        def of_place(place, _):
            own_copy(unit, place).wait_send()
            other_copy(unit, place).wait_send()
            relay_copy(unit, place).wait_send()
            return 0

        return lax.fori_loop(0, LONG, of_place, 0)

    lax.fori_loop(0, 3, drain, 0)
    for batch in range(2):
        for place in range(LONG):
            part_copy(batch, place).wait_send()
            sum_copy(batch, place).wait_send()
            back_copy(batch, place).wait_send()
        for copy in aside_copies(batch):
            copy.wait_send()
        for step in range(STEPS):
            out_copy(batch, step).wait()


def body(
    tokens_fwd,
    expert_ids_fwd,
    route_weights_fwd,
    tokens_bwd,
    cotangent,
    expert_ids_bwd,
    route_weights_bwd,
    w_gate,
    w_up,
    w_down,
):
    anywhere = pl.BlockSpec(memory_space=pl.ANY)
    vmem = pl.BlockSpec(memory_space=pltpu.VMEM)
    out = jax.ShapeDtypeStruct((1, TOK, WIDTH), BF16)
    block = (LONG, CAP, WIDTH)

    def sems(*shape):
        return [pltpu.SemaphoreType.DMA(shape), pltpu.SemaphoreType.DMA(shape)]

    return pl.pallas_call(
        kernel,
        out_shape=(out, out),
        in_specs=[anywhere] * 3 + [vmem] * 4 + [anywhere] * 3,
        out_specs=(anywhere, anywhere),
        scratch_shapes=[
            pltpu.VMEM((3, TOK, WIDTH), BF16),
            pltpu.VMEM((3, 2) + block, BF16),
            pltpu.VMEM((3, 5) + block, BF16),
            pltpu.VMEM((2,) + block, BF16),
            pltpu.VMEM((2, 2) + block, BF16),
            pltpu.VMEM((2,) + block, F32),
            pltpu.VMEM((2, 2) + block, BF16),
            pltpu.VMEM((2, 2) + block, BF16),
            pltpu.VMEM((WIDTH, HIDDEN), BF16),
            pltpu.VMEM((WIDTH, HIDDEN), BF16),
            pltpu.VMEM((HIDDEN, WIDTH), BF16),
            pltpu.VMEM((2, GROUPS, 8 * CAP, HIDDEN), F32),
            pltpu.VMEM((2, TOK, WIDTH), BF16),
            pltpu.VMEM((2, TOK), jnp.int32),
            pltpu.VMEM((2, TOK), jnp.int32),
            pltpu.VMEM((2, TOK), F32),
            pltpu.VMEM((2, TOK), F32),
            pltpu.SemaphoreType.DMA((6,)),
            *sems(3, LONG),
            *sems(3, LONG),
            *sems(3, LONG),
            *sems(3, LONG),
            *sems(2, LONG),
            *sems(2, LONG),
            *sems(2, LONG),
            *sems(2, 3),
            pltpu.SemaphoreType.DMA((2, STEPS)),
        ],
        compiler_params=pltpu.CompilerParams(
            collective_id=0, has_side_effects=True, vmem_limit_bytes=62 * 2**20
        ),
        name="relay_experts",
    )(
        tokens_fwd,
        tokens_bwd,
        cotangent,
        expert_ids_fwd[0].T,
        expert_ids_bwd[0].T,
        route_weights_fwd[0].T,
        route_weights_bwd[0].T,
        w_gate,
        w_up,
        w_down,
    )


def solution(mesh):
    rows = P("section", "expert", None)
    columns = P("section", None, "expert")
    in_specs = (rows,) * 7 + (columns, columns, rows)
    return jax.shard_map(
        body, mesh=mesh, in_specs=in_specs, out_specs=(rows, rows), check_vma=False
    )
```

```python
import jax
import jax.numpy as jnp
from jax import lax
from jax.experimental import pallas as pl
from jax.experimental.pallas import tpu as pltpu
from jax.sharding import PartitionSpec as P

MESH = pl.DeviceIdType.MESH
BF16 = jnp.bfloat16
F32 = jnp.float32

WIDTH = 4096
HIDDEN = 384
TOK = 96
CAP = 16
SECTIONS = 8
EXPERTS = 16
LONG = 8
SHORT = 4
PARTS = 4
PIECES = LONG + PARTS - 1
GROUPS = 4
COLS = 512
STEPS = WIDTH // COLS
NT = (((1,), (1,)), ((), ()))

OTHER, OWN, ACROSS, PARTNER, DIAGONAL = range(5)

PACK, SEND, ARRIVE, RELAY, FORWARD, RECOMPUTE, BACKWARD, PARTIAL, SUM, BACK, FINISH = range(11)
ORDER = (
    (ARRIVE, 0, 0), (SEND, 0, 1), (SEND, 0, 2), (PACK, 1), (ARRIVE, 1, 0), (PACK, 2), (SEND, 0, 6),
    (SEND, 0, 4), (SEND, 0, 5), (RELAY, 0, 0), (SEND, 0, 3), (SEND, 0, 7), (ARRIVE, 2, 0),
    (RELAY, 1, 0), (ARRIVE, 0, 1), (ARRIVE, 0, 2), (RELAY, 2, 0), (SEND, 1, 3), (SEND, 2, 4),
    (RELAY, 0, 1), (RELAY, 0, 2), (SEND, 1, 5), (SEND, 1, 4), (ARRIVE, 0, 5), (ARRIVE, 0, 6),
    (FORWARD, 0), (PARTIAL, 0, 1), (PARTIAL, 0, 0), (PARTIAL, 0, 8), (PARTIAL, 0, 9),
    (PARTIAL, 0, 10), (RELAY, 0, 5), (RELAY, 0, 6), (SEND, 2, 6), (ARRIVE, 0, 3), (ARRIVE, 0, 4),
    (SEND, 1, 7), (SUM, 0, 1), (SUM, 0, 0), (RELAY, 0, 3), (SUM, 0, 8), (SUM, 0, 9), (RELAY, 0, 4),
    (SUM, 0, 10), (BACK, 0, 1), (ARRIVE, 0, 7), (BACK, 0, 0), (BACK, 0, 8), (BACK, 0, 9),
    (BACK, 0, 10), (RELAY, 0, 7), (SEND, 2, 5), (ARRIVE, 1, 3), (ARRIVE, 2, 4), (FORWARD, 1),
    (PARTIAL, 0, 2), (PARTIAL, 0, 3), (SEND, 1, 6), (FORWARD, 2), (PARTIAL, 0, 4), (PARTIAL, 0, 5),
    (RELAY, 1, 3), (RELAY, 2, 4), (FORWARD, 3), (PARTIAL, 0, 6), (PARTIAL, 0, 7), (ARRIVE, 1, 4),
    (SEND, 2, 7), (ARRIVE, 1, 5), (RELAY, 1, 4), (SUM, 0, 2), (RELAY, 1, 5), (SEND, 2, 3),
    (SUM, 0, 3), (BACK, 0, 2), (ARRIVE, 2, 6), (SUM, 0, 4), (BACK, 0, 3), (RELAY, 2, 6),
    (SEND, 1, 2), (SUM, 0, 5), (BACK, 0, 4), (ARRIVE, 1, 7), (BACK, 0, 5), (RELAY, 1, 7),
    (SUM, 0, 6), (ARRIVE, 2, 5), (SEND, 2, 2), (SUM, 0, 7), (BACK, 0, 6), (ARRIVE, 1, 6),
    (RELAY, 2, 5), (BACK, 0, 7), (RELAY, 1, 6), (RECOMPUTE, 2), (ARRIVE, 2, 7), (RELAY, 2, 7),
    (ARRIVE, 2, 3), (SEND, 1, 1), (RELAY, 2, 3), (ARRIVE, 1, 2), (SEND, 2, 1), (RELAY, 1, 2),
    (BACKWARD, 2), (RECOMPUTE, 3), (PARTIAL, 1, 4), (PARTIAL, 1, 5), (BACKWARD, 3),
    (PARTIAL, 1, 6), (PARTIAL, 1, 7), (ARRIVE, 2, 2), (RELAY, 2, 2), (RECOMPUTE, 1), (SUM, 1, 4),
    (SUM, 1, 5), (BACK, 1, 4), (ARRIVE, 1, 1), (SUM, 1, 6), (BACK, 1, 5), (ARRIVE, 2, 1),
    (FINISH, 0), (RELAY, 1, 1), (SUM, 1, 7), (BACK, 1, 6), (RELAY, 2, 1), (BACKWARD, 1),
    (PARTIAL, 1, 3), (PARTIAL, 1, 2), (BACK, 1, 7), (RECOMPUTE, 0), (BACKWARD, 0), (PARTIAL, 1, 1),
    (PARTIAL, 1, 0), (PARTIAL, 1, 8), (PARTIAL, 1, 9), (PARTIAL, 1, 10), (SUM, 1, 3), (SUM, 1, 2),
    (BACK, 1, 3), (SUM, 1, 1), (BACK, 1, 2), (SUM, 1, 0), (SUM, 1, 8), (SUM, 1, 9), (SUM, 1, 10),
    (BACK, 1, 1), (BACK, 1, 0), (BACK, 1, 8), (BACK, 1, 9), (BACK, 1, 10), (FINISH, 1),
)
ASIDE = 12


def piece_of(piece):
    if 0 < piece < LONG:
        return piece, 0, WIDTH
    return 0, max(piece - LONG + 1, 0) * (WIDTH // PARTS), WIDTH // PARTS


def kernel(
    tok_f,
    tok_b,
    cot,
    ids_f,
    ids_b,
    weights_f,
    weights_b,
    gate_hbm,
    up_hbm,
    down_hbm,
    out_f,
    out_b,
    source,
    pack,
    rows,
    part_f,
    part_in,
    part_own,
    sums,
    back,
    w_gate,
    w_up,
    w_down,
    factors,
    residual,
    ids_in_f,
    ids_in_b,
    weights_in_f,
    weights_in_b,
    load_sem,
    z_send,
    z_recv,
    own_send,
    own_recv,
    other_send,
    other_recv,
    relay_send,
    relay_recv,
    part_send,
    part_recv,
    sum_send,
    sum_recv,
    back_send,
    back_recv,
    aside_send,
    aside_recv,
    out_sem,
):
    section = lax.axis_index("section")
    expert = lax.axis_index("expert")
    z, y = expert // SHORT, expert % SHORT
    base = expert - y
    pair = y // 2
    partner = {"expert": base + (y + 1 - 2 * (y % 2))}
    across = {"expert": base + (SHORT - 1 - y)}

    def along_z(offset):
        return {"expert": lax.rem(z + offset, LONG) * SHORT + y}

    def next_section(batch, offset):
        ahead = 1 if batch == 0 else SECTIONS - 1
        return {"section": lax.rem(section + ahead, SECTIONS)} | along_z(offset)

    loads = [
        pltpu.make_async_copy(tok_f.at[0], source.at[0], load_sem.at[0]),
        pltpu.make_async_copy(tok_b.at[0], source.at[1], load_sem.at[1]),
        pltpu.make_async_copy(cot.at[0], source.at[2], load_sem.at[2]),
        pltpu.make_async_copy(gate_hbm.at[0], w_gate, load_sem.at[3]),
        pltpu.make_async_copy(up_hbm.at[0], w_up, load_sem.at[4]),
        pltpu.make_async_copy(down_hbm.at[0], w_down, load_sem.at[5]),
    ]
    for load in loads:
        load.start()

    barrier = pltpu.get_barrier_semaphore()
    peers = [along_z(offset) for offset in range(1, LONG)]
    peers += [partner, across]
    peers += [next_section(batch, offset) for batch in range(2) for offset in range(LONG)]
    for peer in peers:
        pl.semaphore_signal(barrier, inc=1, device_id=peer, device_id_type=MESH)

    def ahead_of(place):
        half = (place + 1) // 2
        return half + (place + 1) % 2 * (LONG - 2 * half)

    def z_copy(unit, place):
        return pltpu.make_async_remote_copy(
            pack.at[unit, :, place],
            rows.at[unit, pl.ds(OTHER, 2), place],
            z_send.at[unit, place],
            z_recv.at[unit, place],
            device_id=along_z(ahead_of(place)),
            device_id_type=MESH,
        )

    def y_copy(unit, place, plane, to_plane, send, recv, device):
        return pltpu.make_async_remote_copy(
            rows.at[unit, plane, place],
            rows.at[unit, to_plane, place],
            send.at[unit, place],
            recv.at[unit, place],
            device_id=device,
            device_id_type=MESH,
        )

    def own_copy(unit, place):
        return y_copy(unit, place, OWN, PARTNER, own_send, own_recv, partner)

    def other_copy(unit, place):
        return y_copy(unit, place, OTHER, ACROSS, other_send, other_recv, across)

    def relay_copy(unit, place):
        return y_copy(unit, place, ACROSS, DIAGONAL, relay_send, relay_recv, partner)

    def part_copy(batch, piece):
        place, first, width = piece_of(piece)
        cols = pl.ds(first, width)
        src = part_f.at[:, place, :, cols] if batch == 0 else pack.at[1, :, place, :, cols]
        return pltpu.make_async_remote_copy(
            src,
            part_in.at[batch, :, place, :, cols],
            part_send.at[batch, piece],
            part_recv.at[batch, piece],
            device_id=partner,
            device_id_type=MESH,
        )

    def sum_copy(batch, piece):
        place, first, width = piece_of(piece)
        cols = pl.ds(first, width)
        return pltpu.make_async_remote_copy(
            pack.at[2 * batch, 0, place, :, cols],
            sums.at[batch, OTHER, place, :, cols],
            sum_send.at[batch, piece],
            sum_recv.at[batch, piece],
            device_id=across,
            device_id_type=MESH,
        )

    def back_copy(batch, piece):
        place, first, width = piece_of(piece)
        cols = pl.ds(first, width)
        return pltpu.make_async_remote_copy(
            sums.at[batch, :, place, :, cols],
            back.at[batch, :, place, :, cols],
            back_send.at[batch, piece],
            back_recv.at[batch, piece],
            device_id=next_section(batch, LONG - ahead_of(place)),
            device_id_type=MESH,
        )

    def aside_copies(batch):
        pairs = (
            ((tok_f, cot)[batch].at[0], residual.at[batch]),
            ((ids_f, ids_b)[batch], (ids_in_f, ids_in_b)[batch]),
            ((weights_f, weights_b)[batch], (weights_in_f, weights_in_b)[batch]),
        )
        return [
            pltpu.make_async_remote_copy(
                src,
                dst,
                aside_send.at[batch, i],
                aside_recv.at[batch, i],
                device_id=next_section(batch, 0),
                device_id_type=MESH,
            )
            for i, (src, dst) in enumerate(pairs)
        ]

    def out_copy(batch, step):
        cols = pl.ds(pl.multiple_of(step * COLS, COLS), COLS)
        return pltpu.make_async_copy(
            residual.at[batch, :, cols],
            (out_f, out_b)[batch].at[0, :, cols],
            out_sem.at[batch, step],
        )

    def tables(ids):
        names = lax.broadcasted_iota(jnp.int32, (EXPERTS, TOK), 0)
        chosen = [(ids[k : k + 1, :] == names).astype(F32) for k in range(2)]
        earlier = lax.broadcasted_iota(jnp.int32, (TOK, TOK), 0) < lax.broadcasted_iota(
            jnp.int32, (TOK, TOK), 1
        )
        rank = jnp.dot(
            (chosen[0] + chosen[1]).astype(BF16),
            earlier.astype(F32).astype(BF16),
            preferred_element_type=F32,
        )
        ahead = (names >> 1) - z
        ahead = jnp.where(ahead < 0, ahead + LONG, ahead)
        place = jnp.where(ahead > 4, 2 * (LONG - ahead), 2 * ahead - 1)
        place = jnp.where(ahead == 0, 0, place)
        plane = jnp.where((names & 1) == pair, OWN, OTHER)
        slots = (plane * (LONG * CAP) + place * CAP).astype(F32) + rank
        every = lax.broadcasted_iota(jnp.int32, (2 * LONG * CAP, TOK), 0).astype(F32)
        return [
            (jnp.sum(hot * slots, axis=0, keepdims=True) == every).astype(F32) for hot in chosen
        ]

    def pack_rows(unit, table):
        def step(i, _):
            cols = pl.ds(pl.multiple_of(i * COLS, COLS), COLS)
            packed = jnp.dot(table, source[unit, :, cols], preferred_element_type=F32)
            packed = packed.astype(BF16).reshape(2, LONG, CAP, COLS)
            pack[unit, :, :, :, cols] = packed
            rows[unit, OTHER : OWN + 1, 0, :, cols] = packed[:, 0]
            return 0

        lax.fori_loop(0, STEPS, step, 0)

    loads[0].wait()
    pack_rows(0, sum(tables(ids_f)).astype(BF16))
    pl.semaphore_wait(barrier, len(peers))

    def expert_rows(unit, group):
        block = rows[unit, OWN : DIAGONAL + 1, pl.ds(2 * group, 2)]
        return block.reshape(4 * 2 * CAP, WIDTH)

    def pack_unit(unit):
        loads[unit].wait()
        pack_rows(unit, sum(tables(ids_b)).astype(BF16))

    def arrive(unit, place):
        if place > 0:
            z_copy(unit, place).wait_recv()
        own_copy(unit, place).start()
        other_copy(unit, place).start()

    def relay(unit, place):
        other_copy(unit, place).wait_recv()
        relay_copy(unit, place).start()

    def wait_rows(unit, group):
        for place in (2 * group, 2 * group + 1):
            own_copy(unit, place).wait_recv()
            relay_copy(unit, place).wait_recv()

    def keep_partial(value, group, part, cols):
        span = pl.ds(2 * group, 2)
        value = value.reshape(2, 2, 2, CAP, COLS)
        part[:, span, :, cols] = value[1].astype(BF16)
        part_own[:, span, :, cols] = value[0]

    def forward(group):
        wait_rows(0, group)
        block = expert_rows(0, group)
        gate = jnp.dot(block, w_gate[...], preferred_element_type=F32)
        up = jnp.dot(block, w_up[...], preferred_element_type=F32)
        hidden = (gate * jax.nn.sigmoid(gate) * up).astype(BF16)

        def step(i, _):
            cols = pl.ds(pl.multiple_of(i * COLS, COLS), COLS)
            value = jnp.dot(hidden, w_down[:, cols], preferred_element_type=F32)
            keep_partial(value, group, part_f, cols)
            return 0

        lax.fori_loop(0, STEPS, step, 0)

    def recompute(group):
        wait_rows(1, group)
        block = expert_rows(1, group)
        gate = jnp.dot(block, w_gate[...], preferred_element_type=F32)
        up = jnp.dot(block, w_up[...], preferred_element_type=F32)
        q = jax.nn.sigmoid(gate)
        factors[0, group] = up * (q * (1.0 + gate * (1.0 - q)))
        factors[1, group] = gate * q

    def packed_has_left(unit, place):
        if place > 0:
            z_copy(unit, place).wait_send()

    def backward(group):
        wait_rows(2, group)
        packed_has_left(1, 2 * group)
        packed_has_left(1, 2 * group + 1)
        block = expert_rows(2, group)
        grad = lax.dot_general(block, w_down[...], NT, preferred_element_type=F32)
        grad_gate = (grad * factors[0, group]).astype(BF16)
        grad_up = (grad * factors[1, group]).astype(BF16)

        def step(i, _):
            cols = pl.ds(pl.multiple_of(i * COLS, COLS), COLS)
            value = lax.dot_general(grad_gate, w_gate[cols, :], NT, preferred_element_type=F32)
            value += lax.dot_general(grad_up, w_up[cols, :], NT, preferred_element_type=F32)
            keep_partial(value, group, pack.at[1], cols)
            return 0

        lax.fori_loop(0, STEPS, step, 0)

    def add_partials(batch, piece):
        place, first, width = piece_of(piece)
        part_copy(batch, piece).wait_recv()
        if piece < LONG:
            packed_has_left(2 * batch, place)

        def step(i, _):
            cols = pl.ds(pl.multiple_of(first + i * COLS, COLS), COLS)
            total = part_own[:, place, :, cols] + part_in[batch, :, place, :, cols].astype(F32)
            sums[batch, OWN, place, :, cols] = total[0].astype(BF16)
            pack[2 * batch, 0, place, :, cols] = total[1].astype(BF16)
            return 0

        lax.fori_loop(0, width // COLS, step, 0)
        sum_copy(batch, piece).start()

    def send_back(batch, piece):
        sum_copy(batch, piece).wait_recv()
        back_copy(batch, piece).start()

    def finish(batch):
        for copy in aside_copies(batch):
            copy.wait_recv()
        weights = (weights_in_f, weights_in_b)[batch]
        picks = [hot.T.astype(BF16) for hot in tables((ids_in_f, ids_in_b)[batch])]
        same = lax.broadcasted_iota(jnp.int32, (TOK, TOK), 0) == lax.broadcasted_iota(
            jnp.int32, (TOK, TOK), 1
        )
        scale = [
            jnp.sum(jnp.where(same, weights[k : k + 1, :], 0.0), axis=1, keepdims=True)
            for k in range(2)
        ]
        for piece in range(PIECES):
            back_copy(batch, piece).wait_recv()

        def step(i, _):
            cols = pl.ds(pl.multiple_of(i * COLS, COLS), COLS)
            returned = back[batch, :, :, :, cols].reshape(2 * LONG * CAP, COLS)
            first = jnp.dot(picks[0], returned, preferred_element_type=F32)
            second = jnp.dot(picks[1], returned, preferred_element_type=F32)
            total = scale[0] * first + scale[1] * second
            total += residual[batch, :, cols].astype(F32)
            residual[batch, :, cols] = total.astype(BF16)
            out_copy(batch, i).start()
            return 0

        lax.fori_loop(0, STEPS, step, 0)

    run = {
        PACK: pack_unit,
        SEND: lambda unit, place: z_copy(unit, place).start(),
        ARRIVE: arrive,
        RELAY: relay,
        FORWARD: forward,
        RECOMPUTE: recompute,
        BACKWARD: backward,
        PARTIAL: lambda batch, piece: part_copy(batch, piece).start(),
        SUM: add_partials,
        BACK: send_back,
        FINISH: finish,
    }
    loaded = False
    for count, (kind, *which) in enumerate(ORDER):
        if kind in (FORWARD, RECOMPUTE) and not loaded:
            for load in loads[3:]:
                load.wait()
            loaded = True
        run[kind](*which)
        if count == ASIDE:
            for batch in range(2):
                for copy in aside_copies(batch):
                    copy.start()

    def drain(unit, _):
        def of_place(place, _):
            own_copy(unit, place).wait_send()
            other_copy(unit, place).wait_send()
            relay_copy(unit, place).wait_send()
            return 0

        return lax.fori_loop(0, LONG, of_place, 0)

    lax.fori_loop(0, 3, drain, 0)
    for batch in range(2):
        for piece in range(PIECES):
            part_copy(batch, piece).wait_send()
            sum_copy(batch, piece).wait_send()
            back_copy(batch, piece).wait_send()
        for copy in aside_copies(batch):
            copy.wait_send()
        for step in range(STEPS):
            out_copy(batch, step).wait()


def body(
    tokens_fwd,
    expert_ids_fwd,
    route_weights_fwd,
    tokens_bwd,
    cotangent,
    expert_ids_bwd,
    route_weights_bwd,
    w_gate,
    w_up,
    w_down,
):
    anywhere = pl.BlockSpec(memory_space=pl.ANY)
    vmem = pl.BlockSpec(memory_space=pltpu.VMEM)
    out = jax.ShapeDtypeStruct((1, TOK, WIDTH), BF16)
    block = (LONG, CAP, WIDTH)

    def sems(*shape):
        return [pltpu.SemaphoreType.DMA(shape), pltpu.SemaphoreType.DMA(shape)]

    return pl.pallas_call(
        kernel,
        out_shape=(out, out),
        in_specs=[anywhere] * 3 + [vmem] * 4 + [anywhere] * 3,
        out_specs=(anywhere, anywhere),
        scratch_shapes=[
            pltpu.VMEM((3, TOK, WIDTH), BF16),
            pltpu.VMEM((3, 2) + block, BF16),
            pltpu.VMEM((3, 5) + block, BF16),
            pltpu.VMEM((2,) + block, BF16),
            pltpu.VMEM((2, 2) + block, BF16),
            pltpu.VMEM((2,) + block, F32),
            pltpu.VMEM((2, 2) + block, BF16),
            pltpu.VMEM((2, 2) + block, BF16),
            pltpu.VMEM((WIDTH, HIDDEN), BF16),
            pltpu.VMEM((WIDTH, HIDDEN), BF16),
            pltpu.VMEM((HIDDEN, WIDTH), BF16),
            pltpu.VMEM((2, GROUPS, 8 * CAP, HIDDEN), F32),
            pltpu.VMEM((2, TOK, WIDTH), BF16),
            pltpu.VMEM((2, TOK), jnp.int32),
            pltpu.VMEM((2, TOK), jnp.int32),
            pltpu.VMEM((2, TOK), F32),
            pltpu.VMEM((2, TOK), F32),
            pltpu.SemaphoreType.DMA((6,)),
            *sems(3, LONG),
            *sems(3, LONG),
            *sems(3, LONG),
            *sems(3, LONG),
            *sems(2, PIECES),
            *sems(2, PIECES),
            *sems(2, PIECES),
            *sems(2, 3),
            pltpu.SemaphoreType.DMA((2, STEPS)),
        ],
        compiler_params=pltpu.CompilerParams(
            collective_id=0, has_side_effects=True, vmem_limit_bytes=62 * 2**20
        ),
        name="relay_experts",
    )(
        tokens_fwd,
        tokens_bwd,
        cotangent,
        expert_ids_fwd[0].T,
        expert_ids_bwd[0].T,
        route_weights_fwd[0].T,
        route_weights_bwd[0].T,
        w_gate,
        w_up,
        w_down,
    )


def solution(mesh):
    rows = P("section", "expert", None)
    columns = P("section", None, "expert")
    in_specs = (rows,) * 7 + (columns, columns, rows)
    return jax.shard_map(
        body, mesh=mesh, in_specs=in_specs, out_specs=(rows, rows), check_vma=False
    )
```

```python
import jax
import jax.numpy as jnp
from jax import lax
from jax.experimental import pallas as pl
from jax.experimental.pallas import tpu as pltpu
from jax.sharding import PartitionSpec as P

MESH = pl.DeviceIdType.MESH
BF16 = jnp.bfloat16
F32 = jnp.float32

WIDTH = 4096
HIDDEN = 384
TOK = 96
CAP = 16
SECTIONS = 8
EXPERTS = 16
LONG = 8
SHORT = 4
PARTS = 4
PIECES = LONG + PARTS - 1
GROUPS = 4
COLS = 512
STEPS = WIDTH // COLS
NT = (((1,), (1,)), ((), ()))

OTHER, OWN, ACROSS, PARTNER, DIAGONAL = range(5)

PACK, SEND, ARRIVE, RELAY, FORWARD, RECOMPUTE, BACKWARD, PARTIAL, SUM, BACK, FINISH = range(11)
ORDER = (
    (ARRIVE, 0, 0), (SEND, 0, 2), (SEND, 0, 1), (PACK, 1), (ARRIVE, 1, 0), (PACK, 2),
    (ARRIVE, 2, 0), (SEND, 0, 4), (RELAY, 0, 0), (SEND, 0, 5), (SEND, 0, 6), (SEND, 0, 3),
    (SEND, 0, 7), (RELAY, 1, 0), (SEND, 1, 4), (SEND, 1, 5), (ARRIVE, 0, 2), (ARRIVE, 0, 1),
    (RELAY, 2, 0), (RELAY, 0, 2), (RELAY, 0, 1), (SEND, 2, 4), (ARRIVE, 0, 4), (SEND, 1, 3),
    (RELAY, 0, 4), (ARRIVE, 0, 5), (FORWARD, 0), (PARTIAL, 0, 1), (PARTIAL, 0, 0), (PARTIAL, 0, 8),
    (PARTIAL, 0, 9), (PARTIAL, 0, 10), (RELAY, 0, 5), (SEND, 1, 6), (SEND, 2, 5), (ARRIVE, 0, 6),
    (ARRIVE, 0, 3), (RELAY, 0, 6), (SUM, 0, 1), (SUM, 0, 0), (RELAY, 0, 3), (SUM, 0, 8),
    (SUM, 0, 9), (SEND, 2, 6), (ARRIVE, 0, 7), (SUM, 0, 10), (BACK, 0, 1), (BACK, 0, 0),
    (BACK, 0, 8), (BACK, 0, 9), (FORWARD, 2), (PARTIAL, 0, 4), (PARTIAL, 0, 5), (RELAY, 0, 7),
    (BACK, 0, 10), (SEND, 1, 7), (ARRIVE, 1, 4), (FORWARD, 1), (PARTIAL, 0, 2), (PARTIAL, 0, 3),
    (ARRIVE, 1, 5), (RELAY, 1, 4), (SEND, 2, 7), (ARRIVE, 2, 4), (RELAY, 1, 5), (SUM, 0, 4),
    (RELAY, 2, 4), (ARRIVE, 1, 3), (SUM, 0, 5), (BACK, 0, 4), (FORWARD, 3), (PARTIAL, 0, 6),
    (PARTIAL, 0, 7), (SEND, 2, 3), (RELAY, 1, 3), (BACK, 0, 5), (ARRIVE, 1, 6), (SUM, 0, 2),
    (RELAY, 1, 6), (ARRIVE, 2, 5), (SUM, 0, 3), (BACK, 0, 2), (RELAY, 2, 5), (BACK, 0, 3),
    (SEND, 1, 2), (ARRIVE, 2, 6), (RECOMPUTE, 2), (SEND, 2, 2), (RELAY, 2, 6), (ARRIVE, 1, 7),
    (SUM, 0, 6), (SEND, 1, 1), (RELAY, 1, 7), (SUM, 0, 7), (BACK, 0, 6), (SEND, 2, 1),
    (ARRIVE, 2, 7), (BACK, 0, 7), (RELAY, 2, 7), (ARRIVE, 2, 3), (BACKWARD, 2), (PARTIAL, 1, 4),
    (PARTIAL, 1, 5), (RELAY, 2, 3), (RECOMPUTE, 3), (ARRIVE, 1, 2), (BACKWARD, 3), (ARRIVE, 2, 2),
    (PARTIAL, 1, 7), (PARTIAL, 1, 6), (RELAY, 1, 2), (SUM, 1, 4), (RELAY, 2, 2), (ARRIVE, 1, 1),
    (SUM, 1, 5), (BACK, 1, 4), (RELAY, 1, 1), (ARRIVE, 2, 1), (BACK, 1, 5), (RELAY, 2, 1),
    (SUM, 1, 7), (FINISH, 0), (SUM, 1, 6), (BACK, 1, 7), (RECOMPUTE, 1), (BACKWARD, 1),
    (PARTIAL, 1, 3), (PARTIAL, 1, 2), (BACK, 1, 6), (RECOMPUTE, 0), (BACKWARD, 0), (PARTIAL, 1, 1),
    (PARTIAL, 1, 0), (PARTIAL, 1, 8), (PARTIAL, 1, 9), (PARTIAL, 1, 10), (SUM, 1, 3), (SUM, 1, 2),
    (BACK, 1, 3), (SUM, 1, 1), (BACK, 1, 2), (SUM, 1, 0), (SUM, 1, 8), (SUM, 1, 9), (SUM, 1, 10),
    (BACK, 1, 1), (BACK, 1, 0), (BACK, 1, 8), (BACK, 1, 9), (BACK, 1, 10), (FINISH, 1),
)
ASIDE = 12


def piece_of(piece):
    if 0 < piece < LONG:
        return piece, 0, WIDTH
    return 0, max(piece - LONG + 1, 0) * (WIDTH // PARTS), WIDTH // PARTS


def kernel(
    tok_f,
    tok_b,
    cot,
    ids_f,
    ids_b,
    weights_f,
    weights_b,
    gate_hbm,
    up_hbm,
    down_hbm,
    out_f,
    out_b,
    source,
    pack,
    rows,
    part_f,
    part_in,
    part_own,
    sums,
    back,
    w_gate,
    w_up,
    w_down,
    factors,
    residual,
    ids_in_f,
    ids_in_b,
    weights_in_f,
    weights_in_b,
    load_sem,
    z_send,
    z_recv,
    own_send,
    own_recv,
    other_send,
    other_recv,
    relay_send,
    relay_recv,
    part_send,
    part_recv,
    sum_send,
    sum_recv,
    back_send,
    back_recv,
    aside_send,
    aside_recv,
    out_sem,
):
    section = lax.axis_index("section")
    expert = lax.axis_index("expert")
    z, y = expert // SHORT, expert % SHORT
    base = expert - y
    pair = y // 2
    partner = {"expert": base + (y + 1 - 2 * (y % 2))}
    across = {"expert": base + (SHORT - 1 - y)}

    def along_z(offset):
        return {"expert": lax.rem(z + offset, LONG) * SHORT + y}

    def next_section(batch, offset):
        ahead = 1 if batch == 0 else SECTIONS - 1
        return {"section": lax.rem(section + ahead, SECTIONS)} | along_z(offset)

    loads = [
        pltpu.make_async_copy(tok_f.at[0], source.at[0], load_sem.at[0]),
        pltpu.make_async_copy(tok_b.at[0], source.at[1], load_sem.at[1]),
        pltpu.make_async_copy(cot.at[0], source.at[2], load_sem.at[2]),
        pltpu.make_async_copy(gate_hbm.at[0], w_gate, load_sem.at[3]),
        pltpu.make_async_copy(up_hbm.at[0], w_up, load_sem.at[4]),
        pltpu.make_async_copy(down_hbm.at[0], w_down, load_sem.at[5]),
    ]
    for load in loads:
        load.start()

    barrier = pltpu.get_barrier_semaphore()
    peers = [along_z(offset) for offset in range(1, LONG)]
    peers += [partner, across]
    peers += [next_section(batch, offset) for batch in range(2) for offset in range(LONG)]
    for peer in peers:
        pl.semaphore_signal(barrier, inc=1, device_id=peer, device_id_type=MESH)

    def ahead_of(place):
        half = (place + 1) // 2
        return half + (place + 1) % 2 * (LONG - 2 * half)

    def z_copy(unit, place):
        return pltpu.make_async_remote_copy(
            pack.at[unit, :, place],
            rows.at[unit, pl.ds(OTHER, 2), place],
            z_send.at[unit, place],
            z_recv.at[unit, place],
            device_id=along_z(ahead_of(place)),
            device_id_type=MESH,
        )

    def y_copy(unit, place, plane, to_plane, send, recv, device):
        return pltpu.make_async_remote_copy(
            rows.at[unit, plane, place],
            rows.at[unit, to_plane, place],
            send.at[unit, place],
            recv.at[unit, place],
            device_id=device,
            device_id_type=MESH,
        )

    def own_copy(unit, place):
        return y_copy(unit, place, OWN, PARTNER, own_send, own_recv, partner)

    def other_copy(unit, place):
        return y_copy(unit, place, OTHER, ACROSS, other_send, other_recv, across)

    def relay_copy(unit, place):
        return y_copy(unit, place, ACROSS, DIAGONAL, relay_send, relay_recv, partner)

    def part_copy(batch, piece):
        place, first, width = piece_of(piece)
        cols = pl.ds(first, width)
        src = part_f.at[:, place, :, cols] if batch == 0 else pack.at[1, :, place, :, cols]
        return pltpu.make_async_remote_copy(
            src,
            part_in.at[batch, :, place, :, cols],
            part_send.at[batch, piece],
            part_recv.at[batch, piece],
            device_id=partner,
            device_id_type=MESH,
        )

    def sum_copy(batch, piece):
        place, first, width = piece_of(piece)
        cols = pl.ds(first, width)
        return pltpu.make_async_remote_copy(
            pack.at[2 * batch, 0, place, :, cols],
            sums.at[batch, OTHER, place, :, cols],
            sum_send.at[batch, piece],
            sum_recv.at[batch, piece],
            device_id=across,
            device_id_type=MESH,
        )

    def back_copy(batch, piece):
        place, first, width = piece_of(piece)
        cols = pl.ds(first, width)
        return pltpu.make_async_remote_copy(
            sums.at[batch, :, place, :, cols],
            back.at[batch, :, place, :, cols],
            back_send.at[batch, piece],
            back_recv.at[batch, piece],
            device_id=next_section(batch, LONG - ahead_of(place)),
            device_id_type=MESH,
        )

    def aside_copies(batch):
        pairs = (
            ((tok_f, cot)[batch].at[0], residual.at[batch]),
            ((ids_f, ids_b)[batch], (ids_in_f, ids_in_b)[batch]),
            ((weights_f, weights_b)[batch], (weights_in_f, weights_in_b)[batch]),
        )
        return [
            pltpu.make_async_remote_copy(
                src,
                dst,
                aside_send.at[batch, i],
                aside_recv.at[batch, i],
                device_id=next_section(batch, 0),
                device_id_type=MESH,
            )
            for i, (src, dst) in enumerate(pairs)
        ]

    def out_copy(batch, step):
        cols = pl.ds(pl.multiple_of(step * COLS, COLS), COLS)
        return pltpu.make_async_copy(
            residual.at[batch, :, cols],
            (out_f, out_b)[batch].at[0, :, cols],
            out_sem.at[batch, step],
        )

    def tables(ids):
        names = lax.broadcasted_iota(jnp.int32, (EXPERTS, TOK), 0)
        chosen = [(ids[k : k + 1, :] == names).astype(F32) for k in range(2)]
        earlier = lax.broadcasted_iota(jnp.int32, (TOK, TOK), 0) < lax.broadcasted_iota(
            jnp.int32, (TOK, TOK), 1
        )
        rank = jnp.dot(
            (chosen[0] + chosen[1]).astype(BF16),
            earlier.astype(F32).astype(BF16),
            preferred_element_type=F32,
        )
        ahead = (names >> 1) - z
        ahead = jnp.where(ahead < 0, ahead + LONG, ahead)
        place = jnp.where(ahead > 4, 2 * (LONG - ahead), 2 * ahead - 1)
        place = jnp.where(ahead == 0, 0, place)
        plane = jnp.where((names & 1) == pair, OWN, OTHER)
        slots = (plane * (LONG * CAP) + place * CAP).astype(F32) + rank
        every = lax.broadcasted_iota(jnp.int32, (2 * LONG * CAP, TOK), 0).astype(F32)
        return [
            (jnp.sum(hot * slots, axis=0, keepdims=True) == every).astype(F32) for hot in chosen
        ]

    def pack_rows(unit, table):
        def step(i, _):
            cols = pl.ds(pl.multiple_of(i * COLS, COLS), COLS)
            packed = jnp.dot(table, source[unit, :, cols], preferred_element_type=F32)
            packed = packed.astype(BF16).reshape(2, LONG, CAP, COLS)
            pack[unit, :, :, :, cols] = packed
            rows[unit, OTHER : OWN + 1, 0, :, cols] = packed[:, 0]
            return 0

        lax.fori_loop(0, STEPS, step, 0)

    loads[0].wait()
    pack_rows(0, sum(tables(ids_f)).astype(BF16))
    pl.semaphore_wait(barrier, len(peers))

    def expert_rows(unit, group):
        block = rows[unit, OWN : DIAGONAL + 1, pl.ds(2 * group, 2)]
        return block.reshape(4 * 2 * CAP, WIDTH)

    def pack_unit(unit):
        loads[unit].wait()
        pack_rows(unit, sum(tables(ids_b)).astype(BF16))

    def arrive(unit, place):
        if place > 0:
            z_copy(unit, place).wait_recv()
        own_copy(unit, place).start()
        other_copy(unit, place).start()

    def relay(unit, place):
        other_copy(unit, place).wait_recv()
        relay_copy(unit, place).start()

    def wait_rows(unit, group):
        for place in (2 * group, 2 * group + 1):
            own_copy(unit, place).wait_recv()
            relay_copy(unit, place).wait_recv()

    def keep_partial(value, group, part, cols):
        span = pl.ds(2 * group, 2)
        value = value.reshape(2, 2, 2, CAP, COLS)
        part[:, span, :, cols] = value[1].astype(BF16)
        part_own[:, span, :, cols] = value[0]

    def forward(group):
        wait_rows(0, group)
        block = expert_rows(0, group)
        gate = jnp.dot(block, w_gate[...], preferred_element_type=F32)
        up = jnp.dot(block, w_up[...], preferred_element_type=F32)
        hidden = (gate * jax.nn.sigmoid(gate) * up).astype(BF16)

        def step(i, _):
            cols = pl.ds(pl.multiple_of(i * COLS, COLS), COLS)
            value = jnp.dot(hidden, w_down[:, cols], preferred_element_type=F32)
            keep_partial(value, group, part_f, cols)
            return 0

        lax.fori_loop(0, STEPS, step, 0)

    def recompute(group):
        wait_rows(1, group)
        block = expert_rows(1, group)
        gate = jnp.dot(block, w_gate[...], preferred_element_type=F32)
        up = jnp.dot(block, w_up[...], preferred_element_type=F32)
        q = jax.nn.sigmoid(gate)
        factors[0, group] = up * (q * (1.0 + gate * (1.0 - q)))
        factors[1, group] = gate * q

    def packed_has_left(unit, place):
        if place > 0:
            z_copy(unit, place).wait_send()

    def backward(group):
        wait_rows(2, group)
        packed_has_left(1, 2 * group)
        packed_has_left(1, 2 * group + 1)
        block = expert_rows(2, group)
        grad = lax.dot_general(block, w_down[...], NT, preferred_element_type=F32)
        grad_gate = (grad * factors[0, group]).astype(BF16)
        grad_up = (grad * factors[1, group]).astype(BF16)

        def step(i, _):
            cols = pl.ds(pl.multiple_of(i * COLS, COLS), COLS)
            value = lax.dot_general(grad_gate, w_gate[cols, :], NT, preferred_element_type=F32)
            value += lax.dot_general(grad_up, w_up[cols, :], NT, preferred_element_type=F32)
            keep_partial(value, group, pack.at[1], cols)
            return 0

        lax.fori_loop(0, STEPS, step, 0)

    def add_partials(batch, piece):
        place, first, width = piece_of(piece)
        part_copy(batch, piece).wait_recv()
        if piece < LONG:
            packed_has_left(2 * batch, place)

        def step(i, _):
            cols = pl.ds(pl.multiple_of(first + i * COLS, COLS), COLS)
            total = part_own[:, place, :, cols] + part_in[batch, :, place, :, cols].astype(F32)
            sums[batch, OWN, place, :, cols] = total[0].astype(BF16)
            pack[2 * batch, 0, place, :, cols] = total[1].astype(BF16)
            return 0

        lax.fori_loop(0, width // COLS, step, 0)
        sum_copy(batch, piece).start()

    def send_back(batch, piece):
        sum_copy(batch, piece).wait_recv()
        back_copy(batch, piece).start()

    def finish(batch):
        for copy in aside_copies(batch):
            copy.wait_recv()
        weights = (weights_in_f, weights_in_b)[batch]
        picks = [hot.T.astype(BF16) for hot in tables((ids_in_f, ids_in_b)[batch])]
        same = lax.broadcasted_iota(jnp.int32, (TOK, TOK), 0) == lax.broadcasted_iota(
            jnp.int32, (TOK, TOK), 1
        )
        scale = [
            jnp.sum(jnp.where(same, weights[k : k + 1, :], 0.0), axis=1, keepdims=True)
            for k in range(2)
        ]
        for piece in range(PIECES):
            back_copy(batch, piece).wait_recv()

        def step(i, _):
            cols = pl.ds(pl.multiple_of(i * COLS, COLS), COLS)
            returned = back[batch, :, :, :, cols].reshape(2 * LONG * CAP, COLS)
            first = jnp.dot(picks[0], returned, preferred_element_type=F32)
            second = jnp.dot(picks[1], returned, preferred_element_type=F32)
            total = scale[0] * first + scale[1] * second
            total += residual[batch, :, cols].astype(F32)
            residual[batch, :, cols] = total.astype(BF16)
            out_copy(batch, i).start()
            return 0

        lax.fori_loop(0, STEPS, step, 0)

    run = {
        PACK: pack_unit,
        SEND: lambda unit, place: z_copy(unit, place).start(),
        ARRIVE: arrive,
        RELAY: relay,
        FORWARD: forward,
        RECOMPUTE: recompute,
        BACKWARD: backward,
        PARTIAL: lambda batch, piece: part_copy(batch, piece).start(),
        SUM: add_partials,
        BACK: send_back,
        FINISH: finish,
    }
    loaded = False
    for count, (kind, *which) in enumerate(ORDER):
        if kind in (FORWARD, RECOMPUTE) and not loaded:
            for load in loads[3:]:
                load.wait()
            loaded = True
        run[kind](*which)
        if count == ASIDE:
            for batch in range(2):
                for copy in aside_copies(batch):
                    copy.start()

    def drain(unit, _):
        def of_place(place, _):
            own_copy(unit, place).wait_send()
            other_copy(unit, place).wait_send()
            relay_copy(unit, place).wait_send()
            return 0

        return lax.fori_loop(0, LONG, of_place, 0)

    lax.fori_loop(0, 3, drain, 0)
    for batch in range(2):
        for piece in range(PIECES):
            part_copy(batch, piece).wait_send()
            sum_copy(batch, piece).wait_send()
            back_copy(batch, piece).wait_send()
        for copy in aside_copies(batch):
            copy.wait_send()
        for step in range(STEPS):
            out_copy(batch, step).wait()


def body(
    tokens_fwd,
    expert_ids_fwd,
    route_weights_fwd,
    tokens_bwd,
    cotangent,
    expert_ids_bwd,
    route_weights_bwd,
    w_gate,
    w_up,
    w_down,
):
    anywhere = pl.BlockSpec(memory_space=pl.ANY)
    vmem = pl.BlockSpec(memory_space=pltpu.VMEM)
    out = jax.ShapeDtypeStruct((1, TOK, WIDTH), BF16)
    block = (LONG, CAP, WIDTH)

    def sems(*shape):
        return [pltpu.SemaphoreType.DMA(shape), pltpu.SemaphoreType.DMA(shape)]

    return pl.pallas_call(
        kernel,
        out_shape=(out, out),
        in_specs=[anywhere] * 3 + [vmem] * 4 + [anywhere] * 3,
        out_specs=(anywhere, anywhere),
        scratch_shapes=[
            pltpu.VMEM((3, TOK, WIDTH), BF16),
            pltpu.VMEM((3, 2) + block, BF16),
            pltpu.VMEM((3, 5) + block, BF16),
            pltpu.VMEM((2,) + block, BF16),
            pltpu.VMEM((2, 2) + block, BF16),
            pltpu.VMEM((2,) + block, F32),
            pltpu.VMEM((2, 2) + block, BF16),
            pltpu.VMEM((2, 2) + block, BF16),
            pltpu.VMEM((WIDTH, HIDDEN), BF16),
            pltpu.VMEM((WIDTH, HIDDEN), BF16),
            pltpu.VMEM((HIDDEN, WIDTH), BF16),
            pltpu.VMEM((2, GROUPS, 8 * CAP, HIDDEN), F32),
            pltpu.VMEM((2, TOK, WIDTH), BF16),
            pltpu.VMEM((2, TOK), jnp.int32),
            pltpu.VMEM((2, TOK), jnp.int32),
            pltpu.VMEM((2, TOK), F32),
            pltpu.VMEM((2, TOK), F32),
            pltpu.SemaphoreType.DMA((6,)),
            *sems(3, LONG),
            *sems(3, LONG),
            *sems(3, LONG),
            *sems(3, LONG),
            *sems(2, PIECES),
            *sems(2, PIECES),
            *sems(2, PIECES),
            *sems(2, 3),
            pltpu.SemaphoreType.DMA((2, STEPS)),
        ],
        compiler_params=pltpu.CompilerParams(
            collective_id=0, has_side_effects=True, vmem_limit_bytes=62 * 2**20
        ),
        name="relay_experts",
    )(
        tokens_fwd,
        tokens_bwd,
        cotangent,
        expert_ids_fwd[0].T,
        expert_ids_bwd[0].T,
        route_weights_fwd[0].T,
        route_weights_bwd[0].T,
        w_gate,
        w_up,
        w_down,
    )


def solution(mesh):
    rows = P("section", "expert", None)
    columns = P("section", None, "expert")
    in_specs = (rows,) * 7 + (columns, columns, rows)
    return jax.shard_map(
        body, mesh=mesh, in_specs=in_specs, out_specs=(rows, rows), check_vma=False
    )
```
